512 devices in a mesh: batch: 64 (over y, z), proto: 8 (over x, core).
Axes of the slice: x: 4, y: 4, z: 16, core: 2. Of those that a mesh axis runs over, the one named last changes fastest.
Arguments:
- embeddings: bfloat16 [2, 32768, 256], P(None, 'batch'), may hold values from -0.5 to 0.5
- prototypes: bfloat16 [16384, 256], P('proto'), may hold values from -0.75 to 0.75
Outputs:
- grad_embeddings: float32 [2, 32768, 256], P(None, 'batch')
- grad_prototypes: float32 [16384, 256], P(('proto', 'batch'))
The draws below stay inside these ranges and needn't reach their ends.
All inputs are finite; a program needn't handle non-finite values.
Results may differ from the reference program's by a relative error of at most 0.0069.
Values sent between devices are 32-bit elements; how exact they have to be, the bound alone decides.
A program may use at most 64 MiB of HBM per device.

```python
import math
import jax
import jax.numpy as jnp
from jax import lax

D = 256
ITERS = 3
K = 16384
BATCH = 32768


def draw_prototypes(key, part):
    key = jax.random.fold_in(key, 7)
    entry_key, scale_key = jax.random.split(key)
    entries = jnp.clip(jax.random.normal(entry_key, (K, D), jnp.float32), -4.0, 4.0)
    log_scale = jax.random.uniform(scale_key, (K, 1), jnp.float32, math.log(0.3), math.log(3.0))
    return (entries * jnp.exp(log_scale) / 16.0).astype(jnp.bfloat16)


def steps_of(key, dims, cuts, low, high):
    loudness = 1.0
    for axis_at, blocks in cuts:
        steps = jax.random.uniform(jax.random.fold_in(jax.random.fold_in(key, 6), axis_at), (blocks,), jnp.float32, low / len(cuts), high / len(cuts))
        loudness = loudness * jnp.repeat(jnp.exp(steps), dims[axis_at] // blocks).reshape((-1,) + (1,) * (len(dims) - 1 - axis_at))
    return loudness


def gaussian(rng, shape, width, most, cuts=(), kind=jnp.bfloat16):
    values = jax.random.normal(rng, shape, jnp.float32) * width
    if len(cuts) > 0:
        values = steps_of(rng, shape, cuts, -0.22, 0.18) * values
    return jnp.clip(values, min=-most, max=most).astype(kind)


def setup_inputs(seed: int = 0) -> dict:
    seeds = jax.random.split(jax.random.key(seed), 3)
    embeddings = gaussian(seeds[0], (2, BATCH, D), 0.0625, 0.5, ((1, 64),))
    prototypes = draw_prototypes(jax.random.fold_in(seeds[2], 71), 0)
    return {"embeddings": embeddings, "prototypes": prototypes}


EPS_SINK = 0.05
TEMPER = 0.1

def block_scores(embed_bits, prototypes):
    left_side = embed_bits.astype(jnp.float32)
    right_side = prototypes.astype(jnp.float32)
    return jnp.einsum('vbd,kd->vbk', left_side, right_side)

def reference(embeddings, prototypes):
    widened = embeddings.astype(jnp.float32)
    inverse = 1.0 / jnp.sqrt(lax.optimization_barrier(jnp.sum(widened * widened, axis=-1, keepdims=True)) + 1e-06)
    normed = widened * inverse
    embed_bits = normed.astype(jnp.bfloat16)
    block_rows = math.gcd(BATCH, 1024)
    blocks_all = BATCH // block_rows

    def split_rows(array):
        return array.reshape(2, blocks_all, block_rows, array.shape[-1]).transpose(1, 0, 2, 3)
    bits_blocks = split_rows(embed_bits)
    normed_blocks = split_rows(normed)
    inverse_blocks = split_rows(inverse)

    def column_pass(col_factor, opening):

        def block_step(running, pieces):
            expo_tile = jnp.exp(block_scores(pieces, prototypes) / EPS_SINK)
            if opening:
                weights = jnp.ones(expo_tile.shape[:2], jnp.float32)
            else:
                row_total = lax.optimization_barrier(jnp.sum(expo_tile * col_factor[:, None, :], axis=2))
                weights = 1.0 / (BATCH * row_total)
            return (running + lax.optimization_barrier(jnp.sum(expo_tile * weights[:, :, None], axis=1)), None)
        summed, unused = lax.scan(block_step, jnp.zeros((2, K), jnp.float32), bits_blocks)
        return 1.0 / (K * summed)
    col_factor = column_pass(None, True)
    for repeat in range(ITERS - 1):
        col_factor = column_pass(col_factor, False)

    def final_step(running, pieces):
        bits_piece, normed_piece, inverse_piece = pieces
        scores = block_scores(bits_piece, prototypes)
        expo_tile = jnp.exp(scores / EPS_SINK)
        row_total = lax.optimization_barrier(jnp.sum(expo_tile * col_factor[:, None, :], axis=2))
        targets = expo_tile * col_factor[:, None, :] / row_total[:, :, None]
        soft_tile = jnp.exp(scores / TEMPER)
        predict = soft_tile / lax.optimization_barrier(jnp.sum(soft_tile, axis=2, keepdims=True))
        grad_bits = ((predict - targets[::-1]) / TEMPER).astype(jnp.bfloat16)
        grad_wide = grad_bits.astype(jnp.float32)
        embed_grad = jnp.einsum('vbk,kd->vbd', grad_wide, prototypes.astype(jnp.float32))
        along_unit = lax.optimization_barrier(jnp.sum(normed_piece * embed_grad, axis=-1, keepdims=True))
        grad_piece = inverse_piece * (embed_grad - normed_piece * along_unit)
        running = running + jnp.einsum('vbk,vbd->kd', grad_wide, bits_piece.astype(jnp.float32))
        return (running, grad_piece)
    grad_prototypes, grad_blocks = lax.scan(final_step, jnp.zeros((K, D), jnp.float32), (bits_blocks, normed_blocks, inverse_blocks))
    grad_embeddings = grad_blocks.transpose(1, 0, 2, 3).reshape(2, BATCH, D)
    return (grad_embeddings, grad_prototypes)
```

```python
import functools

import jax
import jax.numpy as jnp
from jax import lax
from jax.experimental import pallas as pl
from jax.experimental.pallas import tpu as pltpu
from jax.sharding import PartitionSpec as P

MESH = pl.DeviceIdType.MESH
F32, BF16 = jnp.float32, jnp.bfloat16
ITERS = 3
NX, NY, NZ = 4, 4, 16
D = 256
ROWS = 1024
HALF = 512
KL = 2048
KY = 512
K_ALL, B_ALL = 16384, 32768


def dot_nt(a, b):
    return lax.dot_general(a, b, (((1,), (1,)), ((), ())), preferred_element_type=F32)


def dot_nn(a, b):
    return jnp.dot(a, b, preferred_element_type=F32)


def two_rows(vec):
    hi = vec.astype(BF16).astype(F32)
    lo = vec - hi
    at = lax.broadcasted_iota(jnp.int32, (16, vec.shape[1]), 0)
    return jnp.where(at == 0, hi, jnp.where(at == 1, lo, 0.0)).astype(BF16)


def lanes(block):
    return jnp.concatenate([block[i : i + 1, :] for i in range(block.shape[0])], axis=1)


def kernel(
    emb_ref, prot_ref, oe_ref, op_ref,
    eb, ef, yg, cg, soft, expo, softt, grads,
    cbuf, fac, yr, zs, zr, ya, rbuf, rr, rowy, rowyr,
    isb, irb, colb,
    part, csend, crecv, xsend, xrecv, outs,
    gp, zb, hs, hr, opb,
    s_small, r_small, s_big, r_big, l_sem,
):
    b_ix, p_ix = lax.axis_index("batch"), lax.axis_index("proto")
    x, c = p_ix // 2, p_ix % 2
    y, z = b_ix // NZ, b_ix % NZ

    def dev(xx, yy, zz, cc):
        return (yy * NZ + zz, xx * 2 + cc)

    def ypeer(j):
        return dev(x, (y + j) % NY, z, c)

    def zpeer(j):
        return dev(x, y, (z + j + NZ) % NZ, c)

    def xpeer(j):
        return dev((x + j) % NX, y, z, c)

    def ppeer(j):
        return dev((x + j // 2) % NX, y, z, (c + j) % 2)

    other = dev(x, y, z, 1 - c)
    sent = []

    def send(src, dst, ssem, rsem, to):
        cp = pltpu.make_async_remote_copy(
            src_ref=src, dst_ref=dst, send_sem=ssem, recv_sem=rsem, device_id=to, device_id_type=MESH
        )
        cp.start()
        return cp

    def wait_bytes(ref, sem):
        pltpu.make_async_copy(ref, ref, sem).wait()

    bar = pltpu.get_barrier_semaphore()
    peers = (
        [zpeer(j) for j in (8, 7, 9, 6, 10, 5, 11, 4, 12, 3, 13, 2, 14, 1, 15)]
        + [ypeer(j) for j in range(1, NY)]
        + [ppeer(j) for j in range(1, 8)]
    )
    for q in peers:
        pl.semaphore_signal(bar, inc=1, device_id=q, device_id_type=MESH)

    def first(i, carry):
        at = pl.ds(pl.multiple_of(i * 128, 128), 128)
        wide = emb_ref[at, :].astype(F32)
        inv = 1.0 / jnp.sqrt(jnp.sum(wide * wide, axis=1, keepdims=True) + 1e-6)
        bits = (wide * inv).astype(BF16)
        eb[0, at, :] = bits
        s = jnp.exp(dot_nt(bits, prot_ref[...]) * 10.0)
        soft[at, :] = s
        grads[at, :] = s.astype(BF16)
        expo[at, :] = (s * s).astype(BF16)
        return carry

    lax.fori_loop(0, 8, first, 0)
    ef[...] = eb[0, pl.ds(pl.multiple_of(c * HALF, HALF), HALF), :].astype(F32)

    def col_pass(it, weights):
        for v in range(2):
            got = dot_nn(weights[v], expo[v * HALF : (v + 1) * HALF, :])
            tot = got[0:1, :] + got[1:2, :]
            for t in range(16):
                cbuf[it, v * 16 + t : v * 16 + t + 1, :] = tot[:, t * 128 : (t + 1) * 128]

    def row_pass(it, at, left, src):
        for v in range(2):
            got = dot_nt(left[v], src[v * HALF : (v + 1) * HALF, :])
            tot = got[0:1, :] + got[1:2, :]
            for t in range(4):
                rbuf[it, at + v * 4 + t : at + v * 4 + t + 1, :] = tot[:, t * 128 : (t + 1) * 128]

    one = [two_rows(jnp.ones((1, HALF), F32))] * 2
    col_pass(0, one)
    pl.semaphore_wait(bar, len(peers))

    def col_exchange(it, meanwhile):
        for j in (2, 1, 3):
            dst_y = (y + j) % NY
            sent.append(send(
                cbuf.at[it, pl.ds(pl.multiple_of(dst_y * 8, 8), 8)], yr.at[it, j - 1],
                s_small.at[it, 0], r_small.at[it, 0], ypeer(j),
            ))
        wait_bytes(yr.at[it], r_small.at[it, 0])
        mine = pl.ds(pl.multiple_of(y * 8, 8), 8)
        zs[it] = cbuf[it, mine, :] + (yr[it, 0] + yr[it, 1] + yr[it, 2])
        for j in (8, 7, 9, 6, 10, 5, 11, 4, 12, 3, 13, 2, 14, 1, 15):
            sent.append(send(zs.at[it], zr.at[it, j - 1], s_small.at[it, 1], r_small.at[it, 1], zpeer(j)))
        meanwhile()
        wait_bytes(zr.at[it], r_small.at[it, 1])
        total = zs[it]
        for j in range(15):
            total = total + zr[it, j]
        ya[it, 3] = total
        for j in (2, 1, 3):
            sent.append(send(ya.at[it, 3], ya.at[it, j - 1], s_small.at[it, 2], r_small.at[it, 2], ypeer(j)))
        wait_bytes(ya.at[it, pl.ds(0, 3)], r_small.at[it, 2])
        for j in range(NY):
            src_y = (y + NY - j) % NY
            fac[it, pl.ds(pl.multiple_of(src_y * 8, 8), 8), :] = 1.0 / (K_ALL * ya[it, (j + 3) % 4])
        return fac[it]

    def row_exchange(it, n, meanwhile):
        for j in (4, 5, 2, 3, 6, 7, 1):
            sent.append(send(
                rbuf.at[it, pl.ds(0, n)], rr.at[it, j - 1, pl.ds(0, n)], s_small.at[it, 3], r_small.at[it, 3], ppeer(j)
            ))
        meanwhile()
        wait_bytes(rr.at[it, :, pl.ds(0, n)], r_small.at[it, 3])
        total = rbuf[it, 0:n]
        for j in range(7):
            total = total + rr[it, j, 0:n]
        return total

    def gather_start():
        for j in (2, 1, 3):
            sent.append(send(ef, yg.at[j - 1], s_big.at[0], r_big.at[0], ypeer(j)))

    def gather_pass_on():
        wait_bytes(yg, r_big.at[0])
        sent.append(send(yg, cg, s_big.at[1], r_big.at[1], other))
        for j in range(3):
            eb[j + 1, pl.ds(pl.multiple_of(c * HALF, HALF), HALF), :] = yg[j].astype(BF16)

    def second_tile():
        wait_bytes(cg, r_big.at[1])
        for j in range(3):
            eb[j + 1, pl.ds(pl.multiple_of((1 - c) * HALF, HALF), HALF), :] = cg[j].astype(BF16)
        own = pl.ds(pl.multiple_of(y * KY, KY), KY)

        def step(i, carry):
            j, h = i // 4, i % 4
            left = eb[j, pl.ds(pl.multiple_of(h * 256, 256), 256), :]
            sc = dot_nt(prot_ref[own, :], left)
            softt[i] = jnp.exp(sc * 10.0)
            return carry

        lax.fori_loop(0, 16, step, 0)

    def nothing():
        pass

    def columns(block, ref):
        turned = block.T
        for i in range(8):
            ref[i * 128 : (i + 1) * 128, :] = jnp.broadcast_to(turned[:, i : i + 1], (128, 128))

    soft_total = None
    colfac = row_total = None
    for it in range(ITERS):
        if it > 0:
            w = 1.0 / (B_ALL * row_total)
            col_pass(it, [two_rows(lanes(w[v * 4 : v * 4 + 4])) for v in range(2)])
        if it == 0:
            def mean_c():
                gather_start()
                row_pass(0, 8, one_k, grads)
            one_k = [two_rows(jnp.ones((1, KL), F32))] * 2
        elif it == 1:
            mean_c = gather_pass_on
        else:
            mean_c = second_tile
        colfac = col_exchange(it, mean_c)
        row_pass(it, 0, [two_rows(lanes(colfac[v * 16 : v * 16 + 16])) for v in range(2)], expo)
        if it == 0:
            both = row_exchange(0, 16, nothing)
            row_total, soft_total = both[0:8], both[8:16]
            rowy[1] = 10.0 / soft_total
        elif it == 1:
            def mean_r():
                columns(rowy[1], isb)
            row_total = row_exchange(it, 8, mean_r)
        else:
            def mean_r():
                for v in range(2):
                    own = fac[2, pl.ds(v * 16 + y * 4, 4), :]
                    turned = jnp.concatenate([own, own], axis=0).T
                    for i in range(4):
                        colb[v, i * 128 : (i + 1) * 128, :] = jnp.broadcast_to(turned[:, i : i + 1], (128, 128))
            row_total = row_exchange(it, 8, mean_r)

    rowy[0] = 10.0 / row_total
    for j in (2, 1, 3):
        sent.append(send(rowy, rowyr.at[j - 1], s_big.at[2], r_big.at[2], ypeer(j)))
    columns(rowy[0], irb)
    col_l = [lanes(colfac[v * 16 : v * 16 + 16]) for v in range(2)]

    core_copies, x_copies = [], []

    def reduce_core(t):
        core_copies[t].wait_recv()
        xsend[t] = part[t] + crecv[t]
        if t < 3:
            x_copies.append(send(xsend.at[t], xrecv.at[t], s_big.at[4], r_big.at[4], xpeer(t + 1)))

    for t in range(4):
        q = (x + t + 1) % NX

        def chunk(i, carry):
            a0 = pl.ds(pl.multiple_of(q * 128 + i * 32, 32), 32)
            a1 = pl.ds(pl.multiple_of(HALF + q * 128 + i * 32, 32), 32)
            s0, s1 = soft[a0, :], soft[a1, :]
            is0, is1 = isb[a0, 0:1], isb[a1, 0:1]
            ir0, ir1 = irb[a0, 0:1], irb[a1, 0:1]
            grads[pl.ds(pl.multiple_of(i * 32, 32), 32), :] = (s0 * is0 - (s1 * s1) * col_l[1] * ir1).astype(BF16)
            grads[pl.ds(pl.multiple_of(128 + i * 32, 32), 32), :] = (s1 * is1 - (s0 * s0) * col_l[0] * ir0).astype(BF16)
            return carry

        lax.fori_loop(0, 4, chunk, 0)
        csend[t] = dot_nn(grads[pl.ds(pl.multiple_of((1 - c) * 128, 128), 128), :], prot_ref[...])
        core_copies.append(send(csend.at[t], crecv.at[t], s_big.at[3], r_big.at[8 + t], other))
        part[t] = dot_nn(grads[pl.ds(pl.multiple_of(c * 128, 128), 128), :], prot_ref[...])
        if t > 0:
            reduce_core(t - 1)

    wait_bytes(rowyr, r_big.at[2])

    def gstep(acc, j, rows_j):
        ir, iss = rows_j
        for h in range(4):
            v, part_h = h // 2, h % 2
            s_own = softt[j * 4 + h]
            s_oth = softt[j * 4 + (2 - 2 * v) + part_h]
            lo = v * 4 + part_h * 2
            lo_o = (1 - v) * 4 + part_h * 2
            is_l = lanes(iss[lo : lo + 2])
            ir_l = lanes(ir[lo_o : lo_o + 2])
            colv = colb[1 - v, :, 0:1]
            g = (s_own * is_l - (s_oth * s_oth) * colv * ir_l).astype(BF16)
            acc = acc + dot_nn(g, eb[j, h * 256 : (h + 1) * 256, :])
        return acc

    acc = jnp.zeros((KY, D), F32)
    for j in range(4):
        src = (rowy[0], rowy[1]) if j == 0 else (rowyr[j - 1, 0], rowyr[j - 1, 1])
        acc = gstep(acc, j, src)
        if j == 0:
            reduce_core(3)
    gp[...] = acc

    def gchunk(j):
        return pl.ds(pl.multiple_of(((z + j + NZ) % NZ) * 32, 32), 32)

    for m in (3, 2, 1):
        sent.append(send(gp.at[gchunk(-m - 5)], zb.at[3 + m - 1], s_big.at[5], r_big.at[12], zpeer(-m)))
    for m in (2, 1):
        sent.append(send(gp.at[gchunk(m + 5)], zb.at[9 + m - 1], s_big.at[5], r_big.at[13], zpeer(m)))
    for m in (3, 2, 1):
        sent.append(send(gp.at[gchunk(-m - 1)], zb.at[m - 1], s_big.at[5], r_big.at[14], zpeer(-m)))
        sent.append(send(gp.at[gchunk(m + 1)], zb.at[6 + m - 1], s_big.at[5], r_big.at[15], zpeer(m)))

    wait_bytes(xrecv, r_big.at[4])
    eg = xsend[3] + (xrecv[0] + xrecv[1] + xrecv[2])
    wide = emb_ref[pl.ds(pl.multiple_of(c * HALF + x * 128, 128), 128), :].astype(F32)
    inv = 1.0 / jnp.sqrt(jnp.sum(wide * wide, axis=1, keepdims=True) + 1e-6)
    normed = wide * inv
    along = jnp.sum(normed * eg, axis=1, keepdims=True)
    outs[0, 0] = inv * (eg - normed * along)
    x_sends = []
    for j in (2, 1, 3):
        x_sends.append(send(outs.at[0, 0], outs.at[0, j], s_big.at[6], r_big.at[16 + j], xpeer(j)))
    fwd = [send(outs.at[0, 0], outs.at[1, 0], s_big.at[7], r_big.at[20], other)]
    local = []

    def keep(slot, j, cc, sem):
        xx = (x + NX - j) % NX
        cp = pltpu.make_async_copy(
            outs.at[slot, j], oe_ref.at[pl.ds(pl.multiple_of(cc * HALF + xx * 128, 128), 128)], l_sem.at[sem]
        )
        cp.start()
        local.append(cp)

    keep(0, 0, c, 0)

    def role(n, lo, cnt, j, sem, to, slot):
        wait_bytes(zb.at[pl.ds(lo, cnt)], r_big.at[sem])
        tot = gp[gchunk(j), :]
        for k in range(cnt):
            tot = tot + zb[lo + k]
        hs[slot] = tot
        sent.append(send(hs.at[slot], hr.at[slot], s_big.at[8], r_big.at[24], zpeer(to)))

    role(0, 3, 3, -5, 12, -5, 1)
    role(0, 9, 2, 5, 13, 5, 3)
    role(0, 0, 3, -1, 14, -1, 0)
    role(0, 6, 3, 1, 15, 1, 2)

    for n, j in enumerate((1, 3, 2)):
        x_sends[(1, 2, 0)[n]].wait_recv()
        fwd.append(send(outs.at[0, j], outs.at[1, j], s_big.at[7], r_big.at[20 + j], other))
        keep(0, j, c, j)
    wait_bytes(hr, r_big.at[24])
    opb[...] = gp[gchunk(0), :] + (hr[0] + hr[1]) + (hr[2] + hr[3])
    last = pltpu.make_async_copy(opb, op_ref, l_sem.at[8])
    last.start()
    for n, j in enumerate((0, 1, 3, 2)):
        fwd[n].wait_recv()
        keep(1, j, 1 - c, 4 + j)
    for cp in sent + core_copies + x_copies + x_sends + fwd:
        cp.wait_send()
    for cp in local + [last]:
        cp.wait()


def per_device(embeddings, prototypes):
    emb = embeddings.reshape(ROWS, D)
    vm = lambda *s, dt=F32: pltpu.VMEM(s, dt)
    dma = pltpu.SemaphoreType.DMA
    scratch = [
        vm(4, ROWS, D, dt=BF16), vm(HALF, D), vm(3, HALF, D), vm(3, HALF, D),
        vm(ROWS, KL), vm(ROWS, KL, dt=BF16), vm(16, KY, 256), vm(ROWS, KL, dt=BF16),
        vm(ITERS, 32, 128), vm(ITERS, 32, 128), vm(ITERS, 3, 8, 128), vm(ITERS, 8, 128), vm(ITERS, 15, 8, 128), vm(ITERS, 4, 8, 128),
        vm(ITERS, 16, 128), vm(ITERS, 7, 16, 128), vm(2, 8, 128), vm(3, 2, 8, 128),
        vm(ROWS, 128), vm(ROWS, 128), vm(2, KY, 128),
        vm(4, 128, D), vm(4, 128, D), vm(4, 128, D), vm(4, 128, D), vm(3, 128, D), vm(2, 4, 128, D),
        vm(KY, D), vm(11, 32, D), vm(4, 32, D), vm(4, 32, D), vm(32, D),
        dma((ITERS, 4)), dma((ITERS, 4)), dma((9,)), dma((25,)), dma((9,)),
    ]
    ge, gpr = pl.pallas_call(
        kernel,
        out_shape=(jax.ShapeDtypeStruct((ROWS, D), F32), jax.ShapeDtypeStruct((32, D), F32)),
        in_specs=[pl.BlockSpec(memory_space=pltpu.VMEM)] * 2,
        out_specs=(pl.BlockSpec(memory_space=pl.ANY), pl.BlockSpec(memory_space=pl.ANY)),
        scratch_shapes=scratch,
        compiler_params=pltpu.CompilerParams(
            collective_id=0, has_side_effects=True, vmem_limit_bytes=58 << 20
        ),
    )(emb, prototypes)
    return ge.reshape(2, HALF, D), gpr


def solution(mesh):
    in_specs = (P(None, "batch", None), P("proto", None))
    out_specs = (P(None, "batch", None), P(("proto", "batch"), None))
    return jax.shard_map(
        per_device, mesh=mesh, in_specs=in_specs, out_specs=out_specs, check_vma=False
    )
```

```python
import functools

import jax
import jax.numpy as jnp
from jax import lax
from jax.experimental import pallas as pl
from jax.experimental.pallas import tpu as pltpu
from jax.sharding import PartitionSpec as P

MESH = pl.DeviceIdType.MESH
F32, BF16 = jnp.float32, jnp.bfloat16
ITERS = 3
NX, NY, NZ = 4, 4, 16
D = 256
ROWS = 1024
HALF = 512
KL = 2048
KY = 512
K_ALL, B_ALL = 16384, 32768


def dot_nt(a, b):
    return lax.dot_general(a, b, (((1,), (1,)), ((), ())), preferred_element_type=F32)


def dot_nn(a, b):
    return jnp.dot(a, b, preferred_element_type=F32)


def two_rows(vec):
    hi = vec.astype(BF16).astype(F32)
    lo = vec - hi
    at = lax.broadcasted_iota(jnp.int32, (16, vec.shape[1]), 0)
    return jnp.where(at == 0, hi, jnp.where(at == 1, lo, 0.0)).astype(BF16)


def lanes(block):
    return jnp.concatenate([block[i : i + 1, :] for i in range(block.shape[0])], axis=1)


def kernel(
    emb_ref, prot_ref, oe_ref, op_ref,
    eb, ef, yg, cg, soft, expo, softt, turned_expo,
    cbuf, fac, yr, zs, zr, ya, rbuf, rr, rowy, rowyr, sofyr, targ, targt,
    isb, irb, colb,
    part, crecv, xsend, xrecv, outs,
    gp, zb, hs, hr, opb,
    s_small, r_small, s_big, r_big, l_sem,
):
    b_ix, p_ix = lax.axis_index("batch"), lax.axis_index("proto")
    x, c = p_ix // 2, p_ix % 2
    y, z = b_ix // NZ, b_ix % NZ

    def dev(xx, yy, zz, cc):
        return (yy * NZ + zz, xx * 2 + cc)

    def ypeer(j):
        return dev(x, (y + j) % NY, z, c)

    def zpeer(j):
        return dev(x, y, (z + j + NZ) % NZ, c)

    def xpeer(j):
        return dev((x + j) % NX, y, z, c)

    def ppeer(j):
        return dev((x + j // 2) % NX, y, z, (c + j) % 2)

    other = dev(x, y, z, 1 - c)
    sent = []

    def send(src, dst, ssem, rsem, to):
        cp = pltpu.make_async_remote_copy(
            src_ref=src, dst_ref=dst, send_sem=ssem, recv_sem=rsem, device_id=to, device_id_type=MESH
        )
        cp.start()
        return cp

    def wait_bytes(ref, sem):
        pltpu.make_async_copy(ref, ref, sem).wait()

    bar = pltpu.get_barrier_semaphore()
    peers = (
        [zpeer(j) for j in (8, 7, 9, 6, 10, 5, 11, 4, 12, 3, 13, 2, 14, 1, 15)]
        + [ypeer(j) for j in range(1, NY)]
        + [ppeer(j) for j in range(1, 8)]
    )
    for q in peers:
        pl.semaphore_signal(bar, inc=1, device_id=q, device_id_type=MESH)

    def norm_rows(i, carry):
        at = pl.ds(pl.multiple_of(i * 256, 256), 256)
        wide = emb_ref[at, :].astype(F32)
        inv = 1.0 / jnp.sqrt(jnp.sum(wide * wide, axis=1, keepdims=True) + 1e-6)
        eb[0, at, :] = (wide * inv).astype(BF16)
        return carry

    lax.fori_loop(0, 4, norm_rows, 0)

    for k in range(8):
        cols = pl.ds(k * 256, 256)
        for v in range(2):
            tot = jnp.zeros((1, 256), F32)
            for h in range(2):
                at = pl.ds(v * HALF + h * 256, 256)
                sc = jnp.exp(dot_nt(eb[0, at, :], prot_ref[cols, :]) * 10.0)
                soft[at, cols] = sc
                ex = sc * sc
                expo[at, cols] = ex.astype(BF16)
                tot = tot + jnp.sum(ex, axis=0, keepdims=True)
            cbuf[0, v * 16 + 2 * k : v * 16 + 2 * k + 1, :] = tot[:, 0:128]
            cbuf[0, v * 16 + 2 * k + 1 : v * 16 + 2 * k + 2, :] = tot[:, 128:256]

    ef[...] = eb[0, pl.ds(pl.multiple_of(c * HALF, HALF), HALF), :].astype(F32)

    def col_pass(it, weights):
        for v in range(2):
            got = dot_nn(weights[v], expo[v * HALF : (v + 1) * HALF, :])
            tot = got[0:1, :] + got[1:2, :]
            for t in range(16):
                cbuf[it, v * 16 + t : v * 16 + t + 1, :] = tot[:, t * 128 : (t + 1) * 128]

    def row_pass(it, left):
        for v in range(2):
            got = dot_nn(left[v], turned_expo[:, v * HALF : (v + 1) * HALF])
            tot = got[0:1, :] + got[1:2, :]
            for t in range(4):
                rbuf[it, v * 4 + t : v * 4 + t + 1, :] = tot[:, t * 128 : (t + 1) * 128]

    def turned_tile():
        for g in range(4):
            at = pl.ds(g * 256, 256)
            tot = jnp.zeros((1, 256), F32)
            for k in range(8):
                sc = jnp.exp(dot_nt(prot_ref[k * 256 : (k + 1) * 256, :], eb[0, at, :]) * 10.0)
                tot = tot + jnp.sum(sc, axis=0, keepdims=True)
                turned_expo[k * 256 : (k + 1) * 256, at] = (sc * sc).astype(BF16)
            rbuf[0, 8 + 2 * g : 9 + 2 * g, :] = tot[:, 0:128]
            rbuf[0, 9 + 2 * g : 10 + 2 * g, :] = tot[:, 128:256]

    pl.semaphore_wait(bar, len(peers))

    def col_exchange(it, meanwhile):
        for j in (2, 1, 3):
            dst_y = (y + j) % NY
            sent.append(send(
                cbuf.at[it, pl.ds(pl.multiple_of(dst_y * 8, 8), 8)], yr.at[it, j - 1],
                s_small.at[it, 0], r_small.at[it, 0], ypeer(j),
            ))
        wait_bytes(yr.at[it], r_small.at[it, 0])
        mine = pl.ds(pl.multiple_of(y * 8, 8), 8)
        zs[it] = cbuf[it, mine, :] + (yr[it, 0] + yr[it, 1] + yr[it, 2])
        for j in (8, 7, 9, 6, 10, 5, 11, 4, 12, 3, 13, 2, 14, 1, 15):
            sent.append(send(zs.at[it], zr.at[it, j - 1], s_small.at[it, 1], r_small.at[it, 1], zpeer(j)))
        meanwhile()
        wait_bytes(zr.at[it], r_small.at[it, 1])
        total = zs[it]
        for j in range(15):
            total = total + zr[it, j]
        ya[it, 3] = total
        for j in (2, 1, 3):
            sent.append(send(ya.at[it, 3], ya.at[it, j - 1], s_small.at[it, 2], r_small.at[it, 2], ypeer(j)))
        wait_bytes(ya.at[it, pl.ds(0, 3)], r_small.at[it, 2])
        for j in range(NY):
            src_y = (y + NY - j) % NY
            fac[it, pl.ds(pl.multiple_of(src_y * 8, 8), 8), :] = 1.0 / (K_ALL * ya[it, (j + 3) % 4])
        return fac[it]

    def row_exchange(it, n, meanwhile):
        for j in (4, 5, 2, 3, 6, 7, 1):
            sent.append(send(
                rbuf.at[it, pl.ds(0, n)], rr.at[it, j - 1, pl.ds(0, n)], s_small.at[it, 3], r_small.at[it, 3], ppeer(j)
            ))
        meanwhile()
        wait_bytes(rr.at[it, :, pl.ds(0, n)], r_small.at[it, 3])
        total = rbuf[it, 0:n]
        for j in range(7):
            total = total + rr[it, j, 0:n]
        return total

    def gather_some(phase, piece):
        lo = piece * 128
        for j in (2, 1, 3):
            sent.append(send(
                ef.at[pl.ds(phase * 256 + lo, 128)], yg.at[phase, j - 1, pl.ds(lo, 128)],
                s_big.at[0], r_big.at[phase], ypeer(j),
            ))

    own_protos = pl.ds(pl.multiple_of(y * KY, KY), KY)

    def tile_steps(places):
        for j, v, h in places:
            sc = dot_nt(prot_ref[own_protos, :], eb[j, v * HALF + h * 256 : v * HALF + (h + 1) * 256, :])
            softt[j * 4 + v * 2 + h] = jnp.exp(sc * 10.0)

    def own_tile():
        tile_steps([(0, v, h) for v in range(2) for h in range(2)])

    def other_tile(h):
        wait_bytes(yg.at[h], r_big.at[h])
        sent.append(send(yg.at[h], cg.at[h], s_big.at[1], r_big.at[5 + h], other))
        for j in range(3):
            eb[j + 1, pl.ds(pl.multiple_of(c * HALF + h * 256, 256), 256), :] = yg[h, j].astype(BF16)
        wait_bytes(cg.at[h], r_big.at[5 + h])
        for j in range(3):
            eb[j + 1, pl.ds(pl.multiple_of((1 - c) * HALF + h * 256, 256), 256), :] = cg[h, j].astype(BF16)

        def step(j, carry):
            tile_steps([(j, 0, h), (j, 1, h)])
            return carry

        lax.fori_loop(1, 4, step, 0)

    def scale_tiles():
        def rows(i, carry):
            for v in range(2):
                at = pl.ds(pl.multiple_of(v * HALF + i * 32, 32), 32)
                sv = soft[at, :]
                targ[at, :] = sv * sv * col_l[v]
                soft[at, :] = sv * isb[at, 0:1]
            return carry

        lax.fori_loop(0, 16, rows, 0)
        for i in range(16):
            j, v, h = i // 4, (i // 2) % 2, i % 2
            iss = rowy[1] if j == 0 else sofyr[j - 1]
            sv = softt[i]
            targt[i] = sv * sv * colb[v, :, 0:1]
            softt[i] = sv * lanes(iss[v * 4 + h * 2 : v * 4 + h * 2 + 2])

    def columns(block, ref):
        turned = block.T
        for i in range(8):
            ref[i * 128 : (i + 1) * 128, :] = jnp.broadcast_to(turned[:, i : i + 1], (128, 128))

    soft_total = None
    colfac = row_total = None
    for it in range(ITERS):
        if it > 0:
            w = 1.0 / (B_ALL * row_total)
            col_pass(it, [two_rows(lanes(w[v * 4 : v * 4 + 4])) for v in range(2)])
        if it == 0:
            def mean_c():
                gather_some(0, 0)

                turned_tile()
                own_tile()
        elif it == 1:
            def mean_c():
                gather_some(1, 0)
                other_tile(0)
        else:
            def mean_c():
                other_tile(1)
        colfac = col_exchange(it, mean_c)
        col_l = [lanes(colfac[v * 16 : v * 16 + 16]) for v in range(2)]
        row_pass(it, [two_rows(col_l[v]) for v in range(2)])
        if it == 0:
            def mean_r():
                gather_some(0, 1)
            both = row_exchange(0, 16, mean_r)
            row_total, soft_total = both[0:8], both[8:16]
            rowy[1] = 10.0 / soft_total
        elif it == 1:
            def mean_r():
                gather_some(1, 1)
                for j in (2, 1, 3):
                    sent.append(send(rowy.at[1], sofyr.at[j - 1], s_big.at[2], r_big.at[7], ypeer(j)))
                columns(rowy[1], isb)
            row_total = row_exchange(it, 8, mean_r)
        else:
            def mean_r():
                for v in range(2):
                    own = fac[2, pl.ds(v * 16 + y * 4, 4), :]
                    turned = jnp.concatenate([own, own], axis=0).T
                    for i in range(4):
                        colb[v, i * 128 : (i + 1) * 128, :] = jnp.broadcast_to(turned[:, i : i + 1], (128, 128))
                wait_bytes(sofyr, r_big.at[7])
                scale_tiles()
            row_total = row_exchange(it, 8, mean_r)

    rowy[0] = 10.0 / row_total
    for j in (2, 1, 3):
        sent.append(send(rowy.at[0], rowyr.at[j - 1], s_big.at[2], r_big.at[2], ypeer(j)))
    columns(rowy[0], irb)

    core_copies, x_copies = [], []

    def reduce_core(t):
        core_copies[t].wait_recv()
        xsend[t] = part[t, c] + crecv[t]
        if t < 3:
            x_copies.append(send(xsend.at[t], xrecv.at[t], s_big.at[4], r_big.at[4], xpeer(t + 1)))

    for t in range(4):
        q = (x + t + 1) % NX

        for v in range(2):
            here = pl.ds(pl.multiple_of(v * HALF + q * 128, 128), 128)
            there = pl.ds(pl.multiple_of((1 - v) * HALF + q * 128, 128), 128)
            last = jnp.concatenate([irb[there, :]] * 16, axis=1)
            g = (soft[here, :] - targ[there, :] * last).astype(BF16)
            part[t, v] = dot_nn(g, prot_ref[...])
        core_copies.append(send(part.at[t, 1 - c], crecv.at[t], s_big.at[3], r_big.at[8 + t], other))
        if t > 0:
            reduce_core(t - 1)

    wait_bytes(rowyr, r_big.at[2])

    def gstep(acc, j, ir):
        for v in range(2):
            for h in range(2):
                lo = (1 - v) * 4 + h * 2
                g = (softt[j * 4 + v * 2 + h] - targt[j * 4 + (1 - v) * 2 + h] * lanes(ir[lo : lo + 2])).astype(BF16)
                at = v * HALF + h * 256
                acc = acc + dot_nn(g, eb[j, at : at + 256, :])
        return acc

    acc = jnp.zeros((KY, D), F32)
    for j in range(4):
        acc = gstep(acc, j, rowy[0] if j == 0 else rowyr[j - 1])
        if j == 0:
            reduce_core(3)
    gp[...] = acc

    def gchunk(j):
        return pl.ds(pl.multiple_of(((z + j + NZ) % NZ) * 32, 32), 32)

    for m in (3, 2, 1):
        sent.append(send(gp.at[gchunk(-m - 5)], zb.at[3 + m - 1], s_big.at[5], r_big.at[12], zpeer(-m)))
    for m in (2, 1):
        sent.append(send(gp.at[gchunk(m + 5)], zb.at[9 + m - 1], s_big.at[5], r_big.at[13], zpeer(m)))
    for m in (3, 2, 1):
        sent.append(send(gp.at[gchunk(-m - 1)], zb.at[m - 1], s_big.at[5], r_big.at[14], zpeer(-m)))
        sent.append(send(gp.at[gchunk(m + 1)], zb.at[6 + m - 1], s_big.at[5], r_big.at[15], zpeer(m)))

    wait_bytes(xrecv, r_big.at[4])
    eg = xsend[3] + (xrecv[0] + xrecv[1] + xrecv[2])
    wide = emb_ref[pl.ds(pl.multiple_of(c * HALF + x * 128, 128), 128), :].astype(F32)
    inv = 1.0 / jnp.sqrt(jnp.sum(wide * wide, axis=1, keepdims=True) + 1e-6)
    normed = wide * inv
    along = jnp.sum(normed * eg, axis=1, keepdims=True)
    outs[0, 0] = inv * (eg - normed * along)
    x_sends = []
    for j in (2, 1, 3):
        x_sends.append(send(outs.at[0, 0], outs.at[0, j], s_big.at[6], r_big.at[16 + j], xpeer(j)))
    fwd = [send(outs.at[0, 0], outs.at[1, 0], s_big.at[7], r_big.at[20], other)]
    local = []

    def keep(slot, j, cc, sem):
        xx = (x + NX - j) % NX
        cp = pltpu.make_async_copy(
            outs.at[slot, j], oe_ref.at[pl.ds(pl.multiple_of(cc * HALF + xx * 128, 128), 128)], l_sem.at[sem]
        )
        cp.start()
        local.append(cp)

    keep(0, 0, c, 0)

    def role(n, lo, cnt, j, sem, to, slot):
        wait_bytes(zb.at[pl.ds(lo, cnt)], r_big.at[sem])
        tot = gp[gchunk(j), :]
        for k in range(cnt):
            tot = tot + zb[lo + k]
        hs[slot] = tot
        sent.append(send(hs.at[slot], hr.at[slot], s_big.at[8], r_big.at[24], zpeer(to)))

    role(0, 3, 3, -5, 12, -5, 1)
    role(0, 9, 2, 5, 13, 5, 3)
    role(0, 0, 3, -1, 14, -1, 0)
    role(0, 6, 3, 1, 15, 1, 2)

    for n, j in enumerate((1, 3, 2)):
        x_sends[(1, 2, 0)[n]].wait_recv()
        fwd.append(send(outs.at[0, j], outs.at[1, j], s_big.at[7], r_big.at[20 + j], other))
        keep(0, j, c, j)
    wait_bytes(hr, r_big.at[24])
    opb[...] = gp[gchunk(0), :] + (hr[0] + hr[1]) + (hr[2] + hr[3])
    last = pltpu.make_async_copy(opb, op_ref, l_sem.at[8])
    last.start()
    for n, j in enumerate((0, 1, 3, 2)):
        fwd[n].wait_recv()
        keep(1, j, 1 - c, 4 + j)
    for cp in sent + core_copies + x_copies + x_sends + fwd:
        cp.wait_send()
    for cp in local + [last]:
        cp.wait()


def per_device(embeddings, prototypes):
    emb = embeddings.reshape(ROWS, D)
    vm = lambda *s, dt=F32: pltpu.VMEM(s, dt)
    dma = pltpu.SemaphoreType.DMA
    scratch = [
        vm(4, ROWS, D, dt=BF16), vm(HALF, D), vm(2, 3, 256, D), vm(2, 3, 256, D),
        vm(ROWS, KL), vm(ROWS, KL, dt=BF16), vm(16, KY, 256), vm(KL, ROWS, dt=BF16),
        vm(ITERS, 32, 128), vm(ITERS, 32, 128), vm(ITERS, 3, 8, 128), vm(ITERS, 8, 128), vm(ITERS, 15, 8, 128), vm(ITERS, 4, 8, 128),
        vm(ITERS, 16, 128), vm(ITERS, 7, 16, 128), vm(2, 8, 128), vm(3, 8, 128), vm(3, 8, 128), vm(ROWS, KL), vm(16, KY, 256),
        vm(ROWS, 128), vm(ROWS, 128), vm(2, KY, 128),
        vm(4, 2, 128, D), vm(4, 128, D), vm(4, 128, D), vm(3, 128, D), vm(2, 4, 128, D),
        vm(KY, D), vm(11, 32, D), vm(4, 32, D), vm(4, 32, D), vm(32, D),
        dma((ITERS, 4)), dma((ITERS, 4)), dma((9,)), dma((25,)), dma((9,)),
    ]
    ge, gpr = pl.pallas_call(
        kernel,
        out_shape=(jax.ShapeDtypeStruct((ROWS, D), F32), jax.ShapeDtypeStruct((32, D), F32)),
        in_specs=[pl.BlockSpec(memory_space=pltpu.VMEM)] * 2,
        out_specs=(pl.BlockSpec(memory_space=pl.ANY), pl.BlockSpec(memory_space=pl.ANY)),
        scratch_shapes=scratch,
        compiler_params=pltpu.CompilerParams(
            collective_id=0, has_side_effects=True, vmem_limit_bytes=60 << 20
        ),
    )(emb, prototypes)
    return ge.reshape(2, HALF, D), gpr


def solution(mesh):
    in_specs = (P(None, "batch", None), P("proto", None))
    out_specs = (P(None, "batch", None), P(("proto", "batch"), None))
    return jax.shard_map(
        per_device, mesh=mesh, in_specs=in_specs, out_specs=out_specs, check_vma=False
    )
```

```python
import functools

import jax
import jax.numpy as jnp
from jax import lax
from jax.experimental import pallas as pl
from jax.experimental.pallas import tpu as pltpu
from jax.sharding import PartitionSpec as P

MESH = pl.DeviceIdType.MESH
F32, BF16 = jnp.float32, jnp.bfloat16
ITERS = 3
NX, NY, NZ = 4, 4, 16
D = 256
ROWS = 1024
HALF = 512
KL = 2048
KY = 512
K_ALL, B_ALL = 16384, 32768


def dot_nt(a, b):
    return lax.dot_general(a, b, (((1,), (1,)), ((), ())), preferred_element_type=F32)


def dot_nn(a, b):
    return jnp.dot(a, b, preferred_element_type=F32)


def two_rows(vec):
    hi = vec.astype(BF16).astype(F32)
    lo = vec - hi
    at = lax.broadcasted_iota(jnp.int32, (16, vec.shape[1]), 0)
    return jnp.where(at == 0, hi, jnp.where(at == 1, lo, 0.0)).astype(BF16)


def lanes(block):
    return jnp.concatenate([block[i : i + 1, :] for i in range(block.shape[0])], axis=1)


def kernel(
    emb_ref, prot_hbm, oe_ref, op_ref,
    eb, ef, yg, cg, soft, expo, softt, turned_expo,
    cbuf, fac, yr, zs, zr, ya, rbuf, rr, rowy, rowyr, sofyr, targ, targt,
    isb, irb, colb,
    part, crecv, xsend, xrecv, outs,
    gp, zb, hs, hr, opb,
    s_small, r_small, s_big, r_big, l_sem, prot_ref,
):
    b_ix, p_ix = lax.axis_index("batch"), lax.axis_index("proto")
    x, c = p_ix // 2, p_ix % 2
    y, z = b_ix // NZ, b_ix % NZ

    def dev(xx, yy, zz, cc):
        return (yy * NZ + zz, xx * 2 + cc)

    def ypeer(j):
        return dev(x, (y + j) % NY, z, c)

    def zpeer(j):
        return dev(x, y, (z + j + NZ) % NZ, c)

    def xpeer(j):
        return dev((x + j) % NX, y, z, c)

    def ppeer(j):
        return dev((x + j // 2) % NX, y, z, (c + j) % 2)

    other = dev(x, y, z, 1 - c)
    sent = []

    def send(src, dst, ssem, rsem, to):
        cp = pltpu.make_async_remote_copy(
            src_ref=src, dst_ref=dst, send_sem=ssem, recv_sem=rsem, device_id=to, device_id_type=MESH
        )
        cp.start()
        return cp

    def wait_bytes(ref, sem):
        pltpu.make_async_copy(ref, ref, sem).wait()

    prot_in = pltpu.make_async_copy(prot_hbm, prot_ref, l_sem.at[9])
    prot_in.start()
    bar = pltpu.get_barrier_semaphore()
    peers = (
        [zpeer(j) for j in (8, 7, 9, 6, 10, 5, 11, 4, 12, 3, 13, 2, 14, 1, 15)]
        + [ypeer(j) for j in range(1, NY)]
        + [ppeer(j) for j in range(1, 8)]
    )
    for q in peers:
        pl.semaphore_signal(bar, inc=1, device_id=q, device_id_type=MESH)

    def norm_rows(i, carry):
        at = pl.ds(pl.multiple_of(i * 256, 256), 256)
        wide = emb_ref[at, :].astype(F32)
        inv = 1.0 / jnp.sqrt(jnp.sum(wide * wide, axis=1, keepdims=True) + 1e-6)
        eb[0, at, :] = (wide * inv).astype(BF16)
        return carry

    lax.fori_loop(0, 4, norm_rows, 0)
    prot_in.wait()

    for k in range(8):
        cols = pl.ds(k * 256, 256)
        for v in range(2):
            tot = jnp.zeros((1, 256), F32)
            for h in range(2):
                at = pl.ds(v * HALF + h * 256, 256)
                sc = jnp.exp(dot_nt(eb[0, at, :], prot_ref[cols, :]) * 10.0)
                soft[at, cols] = sc
                ex = sc * sc
                expo[at, cols] = ex.astype(BF16)
                tot = tot + jnp.sum(ex, axis=0, keepdims=True)
            cbuf[0, v * 16 + 2 * k : v * 16 + 2 * k + 1, :] = tot[:, 0:128]
            cbuf[0, v * 16 + 2 * k + 1 : v * 16 + 2 * k + 2, :] = tot[:, 128:256]


    def col_pass(it, weights):
        for v in range(2):
            got = dot_nn(weights[v], expo[v * HALF : (v + 1) * HALF, :])
            tot = got[0:1, :] + got[1:2, :]
            for t in range(16):
                cbuf[it, v * 16 + t : v * 16 + t + 1, :] = tot[:, t * 128 : (t + 1) * 128]

    def row_pass(it, left):
        for v in range(2):
            got = dot_nn(left[v], turned_expo[:, v * HALF : (v + 1) * HALF])
            tot = got[0:1, :] + got[1:2, :]
            for t in range(4):
                rbuf[it, v * 4 + t : v * 4 + t + 1, :] = tot[:, t * 128 : (t + 1) * 128]

    def turned_tile():
        for g in range(4):
            at = pl.ds(g * 256, 256)
            tot = jnp.zeros((1, 256), F32)
            for k in range(8):
                sc = jnp.exp(dot_nt(prot_ref[k * 256 : (k + 1) * 256, :], eb[0, at, :]) * 10.0)
                tot = tot + jnp.sum(sc, axis=0, keepdims=True)
                turned_expo[k * 256 : (k + 1) * 256, at] = (sc * sc).astype(BF16)
            rbuf[0, 8 + 2 * g : 9 + 2 * g, :] = tot[:, 0:128]
            rbuf[0, 9 + 2 * g : 10 + 2 * g, :] = tot[:, 128:256]

    pl.semaphore_wait(bar, len(peers))

    def col_exchange(it, meanwhile):
        for j in (2, 1, 3):
            dst_y = (y + j) % NY
            sent.append(send(
                cbuf.at[it, pl.ds(pl.multiple_of(dst_y * 8, 8), 8)], yr.at[it, j - 1],
                s_small.at[it, 0], r_small.at[it, 0], ypeer(j),
            ))
        wait_bytes(yr.at[it], r_small.at[it, 0])
        mine = pl.ds(pl.multiple_of(y * 8, 8), 8)
        zs[it] = cbuf[it, mine, :] + (yr[it, 0] + yr[it, 1] + yr[it, 2])
        for j in (8, 7, 9, 6, 10, 5, 11, 4, 12, 3, 13, 2, 14, 1, 15):
            sent.append(send(zs.at[it], zr.at[it, j - 1], s_small.at[it, 1], r_small.at[it, 1], zpeer(j)))
        meanwhile()
        wait_bytes(zr.at[it], r_small.at[it, 1])
        total = zs[it]
        for j in range(15):
            total = total + zr[it, j]
        ya[it, 3] = total
        for j in (2, 1, 3):
            sent.append(send(ya.at[it, 3], ya.at[it, j - 1], s_small.at[it, 2], r_small.at[it, 2], ypeer(j)))
        wait_bytes(ya.at[it, pl.ds(0, 3)], r_small.at[it, 2])
        for j in range(NY):
            src_y = (y + NY - j) % NY
            fac[it, pl.ds(pl.multiple_of(src_y * 8, 8), 8), :] = 1.0 / (K_ALL * ya[it, (j + 3) % 4])
        return fac[it]

    def row_exchange(it, n, meanwhile):
        for j in (4, 5, 2, 3, 6, 7, 1):
            sent.append(send(
                rbuf.at[it, pl.ds(0, n)], rr.at[it, j - 1, pl.ds(0, n)], s_small.at[it, 3], r_small.at[it, 3], ppeer(j)
            ))
        meanwhile()
        wait_bytes(rr.at[it, :, pl.ds(0, n)], r_small.at[it, 3])
        total = rbuf[it, 0:n]
        for j in range(7):
            total = total + rr[it, j, 0:n]
        return total

    def gather_some(phase, piece):
        lo = piece * 128
        for j in (2, 1, 3):
            sent.append(send(
                ef.at[pl.ds(phase * 256 + lo, 128)], yg.at[phase, j - 1, pl.ds(lo, 128)],
                s_big.at[0], r_big.at[phase], ypeer(j),
            ))

    own_protos = pl.ds(pl.multiple_of(y * KY, KY), KY)

    def tile_steps(places):
        for j, v, h in places:
            sc = dot_nt(prot_ref[own_protos, :], eb[j, v * HALF + h * 256 : v * HALF + (h + 1) * 256, :])
            softt[j * 4 + v * 2 + h] = jnp.exp(sc * 10.0)

    def own_tile():
        tile_steps([(0, v, h) for v in range(2) for h in range(2)])

    def other_tile(h):
        wait_bytes(yg.at[h], r_big.at[h])
        sent.append(send(yg.at[h], cg.at[h], s_big.at[1], r_big.at[5 + h], other))
        for j in range(3):
            eb[j + 1, pl.ds(pl.multiple_of(c * HALF + h * 256, 256), 256), :] = yg[h, j].astype(BF16)
        wait_bytes(cg.at[h], r_big.at[5 + h])
        for j in range(3):
            eb[j + 1, pl.ds(pl.multiple_of((1 - c) * HALF + h * 256, 256), 256), :] = cg[h, j].astype(BF16)

        def step(j, carry):
            tile_steps([(j, 0, h), (j, 1, h)])
            return carry

        lax.fori_loop(1, 4, step, 0)

    def scale_tiles():
        def rows(i, carry):
            for v in range(2):
                at = pl.ds(pl.multiple_of(v * HALF + i * 32, 32), 32)
                sv = soft[at, :]
                targ[at, :] = sv * sv * col_l[v]
                soft[at, :] = sv * isb[at, 0:1]
            return carry

        lax.fori_loop(0, 16, rows, 0)
        for i in range(16):
            j, v, h = i // 4, (i // 2) % 2, i % 2
            iss = rowy[1] if j == 0 else sofyr[j - 1]
            sv = softt[i]
            targt[i] = sv * sv * colb[v, :, 0:1]
            softt[i] = sv * lanes(iss[v * 4 + h * 2 : v * 4 + h * 2 + 2])

    def columns(block, ref):
        turned = block.T
        for i in range(8):
            ref[i * 128 : (i + 1) * 128, :] = jnp.broadcast_to(turned[:, i : i + 1], (128, 128))

    soft_total = None
    colfac = row_total = None
    for it in range(ITERS):
        if it > 0:
            w = 1.0 / (B_ALL * row_total)
            col_pass(it, [two_rows(lanes(w[v * 4 : v * 4 + 4])) for v in range(2)])
        if it == 0:
            def mean_c():
                ef[...] = eb[0, pl.ds(pl.multiple_of(c * HALF, HALF), HALF), :].astype(F32)
                gather_some(0, 0)

                turned_tile()
                own_tile()
        elif it == 1:
            def mean_c():
                gather_some(1, 0)
                other_tile(0)
        else:
            def mean_c():
                other_tile(1)
        colfac = col_exchange(it, mean_c)
        col_l = [lanes(colfac[v * 16 : v * 16 + 16]) for v in range(2)]
        row_pass(it, [two_rows(col_l[v]) for v in range(2)])
        if it == 0:
            def mean_r():
                gather_some(0, 1)
            both = row_exchange(0, 16, mean_r)
            row_total, soft_total = both[0:8], both[8:16]
            rowy[1] = 10.0 / soft_total
        elif it == 1:
            def mean_r():
                gather_some(1, 1)
                for j in (2, 1, 3):
                    sent.append(send(rowy.at[1], sofyr.at[j - 1], s_big.at[2], r_big.at[7], ypeer(j)))
                columns(rowy[1], isb)
            row_total = row_exchange(it, 8, mean_r)
        else:
            def mean_r():
                for v in range(2):
                    own = fac[2, pl.ds(v * 16 + y * 4, 4), :]
                    turned = jnp.concatenate([own, own], axis=0).T
                    for i in range(4):
                        colb[v, i * 128 : (i + 1) * 128, :] = jnp.broadcast_to(turned[:, i : i + 1], (128, 128))
                wait_bytes(sofyr, r_big.at[7])
                scale_tiles()
            row_total = row_exchange(it, 8, mean_r)

    rowy[0] = 10.0 / row_total
    for j in (2, 1, 3):
        sent.append(send(rowy.at[0], rowyr.at[j - 1], s_big.at[2], r_big.at[2], ypeer(j)))
    columns(rowy[0], irb)

    core_copies, x_copies = [], []

    def reduce_core(t):
        core_copies[t].wait_recv()
        xsend[t] = part[t, c] + crecv[t]
        if t < 3:
            x_copies.append(send(xsend.at[t], xrecv.at[t], s_big.at[4], r_big.at[4], xpeer(t + 1)))

    for t in range(4):
        q = (x + t + 1) % NX

        for v in range(2):
            here = pl.ds(pl.multiple_of(v * HALF + q * 128, 128), 128)
            there = pl.ds(pl.multiple_of((1 - v) * HALF + q * 128, 128), 128)
            last = jnp.concatenate([irb[there, :]] * 16, axis=1)
            g = (soft[here, :] - targ[there, :] * last).astype(BF16)
            part[t, v] = dot_nn(g, prot_ref[...])
        core_copies.append(send(part.at[t, 1 - c], crecv.at[t], s_big.at[3], r_big.at[8 + t], other))
        if t > 0:
            reduce_core(t - 1)

    wait_bytes(rowyr, r_big.at[2])

    def gstep(acc, j, ir):
        for v in range(2):
            for h in range(2):
                lo = (1 - v) * 4 + h * 2
                g = (softt[j * 4 + v * 2 + h] - targt[j * 4 + (1 - v) * 2 + h] * lanes(ir[lo : lo + 2])).astype(BF16)
                at = v * HALF + h * 256
                acc = acc + dot_nn(g, eb[j, at : at + 256, :])
        return acc

    acc = jnp.zeros((KY, D), F32)
    for j in range(4):
        acc = gstep(acc, j, rowy[0] if j == 0 else rowyr[j - 1])
        if j == 0:
            reduce_core(3)
    gp[...] = acc

    def gchunk(j):
        return pl.ds(pl.multiple_of(((z + j + NZ) % NZ) * 32, 32), 32)

    for m in (3, 2, 1):
        sent.append(send(gp.at[gchunk(-m - 5)], zb.at[3 + m - 1], s_big.at[5], r_big.at[12], zpeer(-m)))
    for m in (2, 1):
        sent.append(send(gp.at[gchunk(m + 5)], zb.at[9 + m - 1], s_big.at[5], r_big.at[13], zpeer(m)))
    for m in (3, 2, 1):
        sent.append(send(gp.at[gchunk(-m - 1)], zb.at[m - 1], s_big.at[5], r_big.at[14], zpeer(-m)))
        sent.append(send(gp.at[gchunk(m + 1)], zb.at[6 + m - 1], s_big.at[5], r_big.at[15], zpeer(m)))

    wait_bytes(xrecv, r_big.at[4])
    eg = xsend[3] + (xrecv[0] + xrecv[1] + xrecv[2])
    wide = emb_ref[pl.ds(pl.multiple_of(c * HALF + x * 128, 128), 128), :].astype(F32)
    inv = 1.0 / jnp.sqrt(jnp.sum(wide * wide, axis=1, keepdims=True) + 1e-6)
    normed = wide * inv
    along = jnp.sum(normed * eg, axis=1, keepdims=True)
    outs[0, 0] = inv * (eg - normed * along)
    x_sends = []
    for j in (2, 1, 3):
        x_sends.append(send(outs.at[0, 0], outs.at[0, j], s_big.at[6], r_big.at[16 + j], xpeer(j)))
    fwd = [send(outs.at[0, 0], outs.at[1, 0], s_big.at[7], r_big.at[20], other)]
    local = []

    def keep(slot, j, cc, sem):
        xx = (x + NX - j) % NX
        cp = pltpu.make_async_copy(
            outs.at[slot, j], oe_ref.at[pl.ds(pl.multiple_of(cc * HALF + xx * 128, 128), 128)], l_sem.at[sem]
        )
        cp.start()
        local.append(cp)

    keep(0, 0, c, 0)

    def role(n, lo, cnt, j, sem, to, slot):
        wait_bytes(zb.at[pl.ds(lo, cnt)], r_big.at[sem])
        tot = gp[gchunk(j), :]
        for k in range(cnt):
            tot = tot + zb[lo + k]
        hs[slot] = tot
        sent.append(send(hs.at[slot], hr.at[slot], s_big.at[8], r_big.at[24], zpeer(to)))

    role(0, 3, 3, -5, 12, -5, 1)
    role(0, 9, 2, 5, 13, 5, 3)
    role(0, 0, 3, -1, 14, -1, 0)
    role(0, 6, 3, 1, 15, 1, 2)

    for n, j in enumerate((1, 3, 2)):
        x_sends[(1, 2, 0)[n]].wait_recv()
        fwd.append(send(outs.at[0, j], outs.at[1, j], s_big.at[7], r_big.at[20 + j], other))
        keep(0, j, c, j)
    wait_bytes(hr, r_big.at[24])
    opb[...] = gp[gchunk(0), :] + (hr[0] + hr[1]) + (hr[2] + hr[3])
    last = pltpu.make_async_copy(opb, op_ref, l_sem.at[8])
    last.start()
    for n, j in enumerate((0, 1, 3, 2)):
        fwd[n].wait_recv()
        keep(1, j, 1 - c, 4 + j)
    for cp in sent + core_copies + x_copies + x_sends + fwd:
        cp.wait_send()
    for cp in local + [last]:
        cp.wait()


def per_device(embeddings, prototypes):
    emb = embeddings.reshape(ROWS, D)
    vm = lambda *s, dt=F32: pltpu.VMEM(s, dt)
    dma = pltpu.SemaphoreType.DMA
    scratch = [
        vm(4, ROWS, D, dt=BF16), vm(HALF, D), vm(2, 3, 256, D), vm(2, 3, 256, D),
        vm(ROWS, KL), vm(ROWS, KL, dt=BF16), vm(16, KY, 256), vm(KL, ROWS, dt=BF16),
        vm(ITERS, 32, 128), vm(ITERS, 32, 128), vm(ITERS, 3, 8, 128), vm(ITERS, 8, 128), vm(ITERS, 15, 8, 128), vm(ITERS, 4, 8, 128),
        vm(ITERS, 16, 128), vm(ITERS, 7, 16, 128), vm(2, 8, 128), vm(3, 8, 128), vm(3, 8, 128), vm(ROWS, KL), vm(16, KY, 256),
        vm(ROWS, 128), vm(ROWS, 128), vm(2, KY, 128),
        vm(4, 2, 128, D), vm(4, 128, D), vm(4, 128, D), vm(3, 128, D), vm(2, 4, 128, D),
        vm(KY, D), vm(11, 32, D), vm(4, 32, D), vm(4, 32, D), vm(32, D),
        dma((ITERS, 4)), dma((ITERS, 4)), dma((9,)), dma((25,)), dma((10,)), vm(KL, D, dt=BF16),
    ]
    ge, gpr = pl.pallas_call(
        kernel,
        out_shape=(jax.ShapeDtypeStruct((ROWS, D), F32), jax.ShapeDtypeStruct((32, D), F32)),
        in_specs=[pl.BlockSpec(memory_space=pltpu.VMEM), pl.BlockSpec(memory_space=pl.ANY)],
        out_specs=(pl.BlockSpec(memory_space=pl.ANY), pl.BlockSpec(memory_space=pl.ANY)),
        scratch_shapes=scratch,
        compiler_params=pltpu.CompilerParams(
            collective_id=0, has_side_effects=True, vmem_limit_bytes=60 << 20
        ),
    )(emb, prototypes)
    return ge.reshape(2, HALF, D), gpr


def solution(mesh):
    in_specs = (P(None, "batch", None), P("proto", None))
    out_specs = (P(None, "batch", None), P(("proto", "batch"), None))
    return jax.shard_map(
        per_device, mesh=mesh, in_specs=in_specs, out_specs=out_specs, check_vma=False
    )
```
